256 devices in a mesh: row: 32 (over y, x, core), col: 8 (over z).
Axes of the slice: x: 4, y: 4, z: 8, core: 2. Of those that a mesh axis runs over, the one named last changes fastest.
Arguments:
- kernel: float32 [20480, 20480], P('row', 'col'), as said below
Outputs:
- factored: float32 [20480, 20480], P('row', 'col')
Inputs may be any that keep to these rules, and one draw needn't show every extreme that they name: `kernel`: in global order symmetric positive definite; its eigenvalues are at least 0.05.
All inputs are finite; a program needn't handle non-finite values.
Results may differ from the reference program's by a relative error of at most 0.0003.
Values sent between devices are 32-bit elements; how exact they have to be, the bound alone decides.
No kernel may reach another device: no remote copies, remote signals or barrier semaphores. Data moves between devices by JAX's collectives and lax.ppermute only.
A program may use at most 128 MiB of HBM per device.

```python
import jax
import jax.numpy as jnp
from jax import lax

NB = 128
FEATURES = 512
N = 20480
N_ROW = 32
N_COL = 8


def element_order(blocks_dev, groups):
    place = jnp.arange(N // NB, dtype=jnp.int32)
    glob = place % blocks_dev * groups + place // blocks_dev
    return (glob[:, None] * NB + jnp.arange(NB, dtype=jnp.int32)[None, :]).reshape(-1)


def draw_kernel(key, part):
    key = jax.random.fold_in(key, 7)
    feat_key, diag_key = jax.random.split(key)
    features = jax.random.randint(feat_key, (N, FEATURES), -4, 5).astype(jnp.float32)
    extra = jnp.exp(jax.random.uniform(diag_key, (N,), jnp.float32, jnp.log(0.05), jnp.log(0.5)))
    row_el = element_order(N // (NB * N_ROW), N_ROW)
    col_el = element_order(N // (NB * N_COL), N_COL)
    row_pos = jnp.argsort(row_el, stable=True).astype(jnp.int32)
    col_pos = jnp.argsort(col_el, stable=True).astype(jnp.int32)
    gram = jnp.dot(features[row_el], features[col_el].T, precision=lax.Precision.HIGHEST) * jnp.float32(1.0 / 4096.0)
    return gram.at[row_pos, col_pos].add(extra)


def setup_inputs(seed: int = 0) -> dict:
    key_list = jax.random.split(jax.random.key(seed), 2)
    kernel = draw_kernel(jax.random.fold_in(key_list[1], 71), 0)
    return dict(kernel=kernel)


def row_global(count, blocks):
    place = jnp.arange(count, dtype=jnp.int32)
    return place % blocks * N_ROW + place // blocks

def col_global(count, blocks):
    place = jnp.arange(count, dtype=jnp.int32)
    return place % blocks * N_COL + place // blocks

def reference(kernel):
    order = kernel.shape[0]
    blocks_r = order // (NB * N_ROW)
    blocks_c = order // (NB * N_COL)
    rows_g = row_global(order // NB, blocks_r)
    cols_g = col_global(order // NB, blocks_c)
    matrix = kernel
    panels = []
    for step in range(2):
        place_r = step % N_ROW * blocks_r + step // N_ROW
        place_c = step % N_COL * blocks_c + step // N_COL
        corner = matrix[place_r * NB:(place_r + 1) * NB, place_c * NB:(place_c + 1) * NB]
        lower = jnp.linalg.cholesky(corner)
        inverse = lax.linalg.triangular_solve(lower, jnp.eye(NB, dtype=lower.dtype), left_side=True, lower=True)
        column = matrix[:, place_c * NB:(place_c + 1) * NB]
        solved = jnp.dot(column, inverse.T, precision=lax.Precision.HIGHEST).reshape(order // NB, NB, NB)
        panel = jnp.where((rows_g < step)[:, None, None], jnp.float32(0.0), jnp.where((rows_g == step)[:, None, None], lower[None], solved))
        glob = panel.reshape(N_ROW, blocks_r, NB, NB).transpose(1, 0, 2, 3).reshape(order // NB, NB, NB)
        by_cols = glob.reshape(blocks_c, N_COL, NB, NB).transpose(1, 0, 2, 3).reshape(order, NB)
        panel = panel.reshape(order, NB)
        matrix = matrix - jnp.dot(panel, by_cols.T, precision=lax.Precision.HIGHEST)
        panels.append((place_c, panel))
    row_mask = jnp.repeat(rows_g < 2, NB)
    col_mask = jnp.repeat(cols_g >= 2, NB)
    result = jnp.where(row_mask[:, None] & col_mask[None, :], jnp.float32(0.0), matrix)
    for place_c, panel in panels:
        result = lax.dynamic_update_slice(result, panel, (0, place_c * NB))
    return result
```

```python
import jax
import jax.numpy as jnp
from jax import lax
from jax.experimental import pallas as pl
from jax.experimental.pallas import tpu as pltpu
from jax.sharding import PartitionSpec as P

NB = 128
HIGHEST = lax.Precision.HIGHEST
F32 = jnp.float32
BF16 = jnp.bfloat16


def bc(v): return jnp.broadcast_to(v,(8,NB))
def eliminate4(full):
    eye=(lax.broadcasted_iota(jnp.int32,(NB,NB),0)==lax.broadcasted_iota(jnp.int32,(NB,NB),1)).astype(F32)
    G=NB//8
    A=[full[8*g:8*g+8,:] for g in range(G)]
    I=[eye[8*g:8*g+8,:] for g in range(G)]
    sub=lax.broadcasted_iota(jnp.int32,(8,NB),0)
    lane=lax.broadcasted_iota(jnp.int32,(8,NB),1)
    outU=[];outW=[]
    for k in range(0,NB,4):
        g0,s=divmod(k,8)
        C=[bc(A[g0][:,k+a:k+a+1]) for a in range(4)]
        D=[[bc(C[a][s+b:s+b+1,:]) if b<=a else None for b in range(4)] for a in range(4)]
        ra=[bc(A[g0][s+b:s+b+1,:]) for b in range(4)]
        ri=[bc(I[g0][s+b:s+b+1,:]) for b in range(4)]
        p00,p10,p11=D[0][0],D[1][0],D[1][1]
        ip=1.0/(p00*p11-p10*p10)
        i00,i10,i11=p11*ip,-p10*ip,p00*ip
        q20,q21,q30,q31=D[2][0],D[2][1],D[3][0],D[3][1]
        t02=i00*q20+i10*q21; t12=i10*q20+i11*q21
        t03=i00*q30+i10*q31; t13=i10*q30+i11*q31
        s22=D[2][2]-(q20*t02+q21*t12)
        s32=D[3][2]-(q30*t02+q31*t12)
        s33=D[3][3]-(q30*t03+q31*t13)
        isd=1.0/(s22*s33-s32*s32)
        j22,j32,j33=s33*isd,-s32*isd,s22*isd
        def solve(r):
            y2=r[2]-(t02*r[0]+t12*r[1])
            y3=r[3]-(t03*r[0]+t13*r[1])
            x2=j22*y2+j32*y3; x3=j32*y2+j33*y3
            x0=(i00*r[0]+i10*r[1])-(t02*x2+t03*x3)
            x1=(i10*r[0]+i11*r[1])-(t12*x2+t13*x3)
            return [x0,x1,x2,x3],y2,y3
        xa,ya2,ya3=solve(ra)
        xi,yi2,yi3=solve(ri)
        for g in range(g0,G):
            if g==g0:
                if s==4: continue
                c=[jnp.where(sub>=4,v,0.0) for v in C]
            else:
                c=[bc(A[g][:,k+a:k+a+1]) for a in range(4)]
            A[g]=A[g]-((c[0]*xa[0]+c[1]*xa[1])+(c[2]*xa[2]+c[3]*xa[3]))
            I[g]=I[g]-((c[0]*xi[0]+c[1]*xi[1])+(c[2]*xi[2]+c[3]*xi[3]))
        def rsq(x):
            r=lax.rsqrt(x); return r*(1.5-0.5*x*r*r)
        def norm2(d00,d10,d11,r0,r1):
            rs0=rsq(d00); l10=d10*rs0; e=d11-l10*l10; rs1=rsq(e)
            return lambda r0,r1:(r0*rs0,(r1-l10*(r0*rs0))*rs1)
        nP=norm2(p00,p10,p11,None,None); nS=norm2(s22,s32,s33,None,None)
        u=[*nP(ra[0],ra[1]),*nS(ya2,ya3)]
        w=[*nP(ri[0],ri[1]),*nS(yi2,yi3)]
        for b in range(4):
            u[b]=jnp.where(lane>=k+b,u[b],0.0)
        if s==0:
            hu,hw=u,w
        else:
            uu=hu+u; ww=hw+w
            ru=uu[7]; rw=ww[7]
            for b in range(6,-1,-1):
                ru=jnp.where(sub==b,uu[b],ru); rw=jnp.where(sub==b,ww[b],rw)
            outU.append(ru); outW.append(rw)
    return jnp.concatenate(outU,0), jnp.concatenate(outW,0)


def mm(a, b):
    return jnp.dot(a, b, precision=HIGHEST, preferred_element_type=F32)


def mmt(a, b):
    return lax.dot_general(a, b, (((1,), (1,)), ((), ())), precision=HIGHEST, preferred_element_type=F32)


def factor_kernel(top, bottom, l_ref, w_ref):
    zero = jnp.zeros((NB, NB), F32)
    u0, w0 = eliminate4(top[:, :NB])
    l10 = mmt(bottom[:, :NB], w0)
    u1, w1 = eliminate4(bottom[:, NB:] - mmt(l10, l10))
    l_ref[:NB, :NB] = u0.T
    l_ref[:NB, NB:] = zero
    l_ref[NB:, :NB] = l10
    l_ref[NB:, NB:] = u1.T
    w_ref[:NB, :NB] = w0
    w_ref[:NB, NB:] = zero
    w_ref[NB:, :NB] = -mm(mm(w1, l10), w0)
    w_ref[NB:, NB:] = w1


def factor(top, bottom):
    return pl.pallas_call(
        factor_kernel, out_shape=[jax.ShapeDtypeStruct((2 * NB, 2 * NB), F32)] * 2, name="factor"
    )(top, bottom)


def split(v):
    hi = v.astype(BF16)
    return hi, (v - hi.astype(F32)).astype(BF16)


def update_kernel(info, k_ref, first_ref, second_ref, b0_ref, b1_ref, l_ref, w_ref, out_ref, rows, rhi, rlo):
    step = pl.program_id(0)
    d, z = info[2], info[3]

    @pl.when(step == 0)
    def _():
        solved = mmt(first_ref[...], w_ref[:, :NB]) + mmt(second_ref[...], w_ref[:, NB:])
        rows[...] = solved
        hi, lo = split(solved)
        rhi[...] = hi
        rlo[...] = lo

        @pl.when(d == 0)
        def _():
            rows[:NB, :] = l_ref[:NB, :]

        @pl.when(d == 1)
        def _():
            rows[:NB, NB:] = l_ref[NB:, NB:]

    cols = mm(w_ref[:, :NB], b0_ref[0]) + mm(w_ref[:, NB:], b1_ref[0])
    chi, clo = split(cols)
    dot = lambda a, b: jnp.dot(a, b, preferred_element_type=F32)
    prod = dot(rhi[...], chi) + (dot(rlo[...], chi) + dot(rhi[...], clo))
    out_ref[...] = k_ref[...] - prod

    @pl.when(d < 2)
    def _():
        out_ref[:NB, :] = jnp.zeros((NB, out_ref.shape[1]), F32)

    @pl.when((step == 0) & (z == 0))
    def _():
        out_ref[:, :NB] = rows[:, :NB]

    @pl.when((step == 0) & (z == 1))
    def _():
        out_ref[:, :NB] = rows[:, NB:]


def update(info, kernel, first, second, b0, b1, low, inv):
    r, c = kernel.shape
    w = c // 4
    whole = lambda shape: pl.BlockSpec(shape, lambda n, s: (0,) * len(shape))
    return pl.pallas_call(
        update_kernel,
        out_shape=jax.ShapeDtypeStruct((r, c), F32),
        grid_spec=pltpu.PrefetchScalarGridSpec(
            num_scalar_prefetch=1,
            grid=(4,),
            in_specs=[
                pl.BlockSpec((r, w), lambda n, s: (0, n)),
                whole((r, NB)),
                whole((r, NB)),
                pl.BlockSpec((1, NB, w), lambda n, s: ((s[0] - n + 4) % 4, 0, 0)),
                pl.BlockSpec((1, NB, w), lambda n, s: ((s[1] - n + 4) % 4, 0, 0)),
                whole((2 * NB, 2 * NB)),
                whole((2 * NB, 2 * NB)),
            ],
            out_specs=pl.BlockSpec((r, w), lambda n, s: (0, n)),
            scratch_shapes=[
                pltpu.VMEM((r, 2 * NB), F32),
                pltpu.VMEM((r, 2 * NB), BF16),
                pltpu.VMEM((r, 2 * NB), BF16),
            ],
        ),
        compiler_params=pltpu.CompilerParams(
            dimension_semantics=("arbitrary",), vmem_limit_bytes=40 * 1024 * 1024
        ),
        cost_estimate=pl.CostEstimate(flops=7_000_000_000, bytes_accessed=16_000_000, transcendentals=0),
        name="update",
    )(info, kernel, first, second, b0, b1, low, inv)


def place(core, p, q):
    return p * 8 + q * 2 if core == 0 else q * 8 + p * 2 + 1


def local(kernel):
    row = lax.axis_index("row")
    z = lax.axis_index("col")
    y, x, core = row // 8, row // 2 % 4, row % 2
    p = jnp.where(core == 0, y, x)
    q = jnp.where(core == 0, x, y)

    gathered = lax.all_gather(kernel[:, :NB], "col", axis=0, tiled=False)
    first, second = gathered[0], gathered[1]

    own = kernel[:NB, :NB]
    other = lax.ppermute(own, ("row", "col"), [(r * 8 + a, r * 8 + 1 - a) for r in (0, 1) for a in (0, 1)])
    corner = jnp.where(z == 0, jnp.concatenate([own, other], 1), jnp.concatenate([other, own], 1))
    got = [
        lax.ppermute(
            corner, ("row", "col"), [(r * 8 + a, r * 8 + b) for r in (0, 1) for a, b in ((0, 8 - n), (1, 1 + n))]
        )
        for n in (1, 2, 3)
    ]
    corner = jnp.where(z < 2, corner, got[0] + got[1] + got[2])

    w = kernel.shape[1] // 4
    quarters = [kernel[:NB, j * w : (j + 1) * w] for j in range(4)]
    got = [
        lax.ppermute(quarters[j], "row", [(place(c, 0, 0), place(c, j, 0)) for c in (0, 1)]) for j in (1, 2, 3)
    ]
    quarter = jnp.where(p == 0, quarters[0], got[0] + got[1] + got[2])
    packed = jnp.concatenate([quarter, corner], 1)
    got = [
        lax.ppermute(packed, "row", [(place(c, j, 0), place(c, j, n)) for c in (0, 1) for j in range(4)])
        for n in (1, 3, 2)
    ]
    packed = jnp.where(q == 0, packed, got[0] + got[1] + got[2])
    got = [
        lax.ppermute(
            packed,
            "row",
            [(place(c, j, i), place(c, (j + n) % 4, i)) for c in (0, 1) for j in range(4) for i in range(4)],
        )
        for n in (1, 2, 3)
    ]
    corner = packed[:, w:]
    for n in (1, 2, 3):
        corner = jnp.where(p == n, got[n - 1][:, w:], corner)
    swap = lambda v: lax.ppermute(v, "row", [(i, i ^ 1) for i in range(32)])
    corner_other = swap(corner)
    top = jnp.where(core == 0, corner, corner_other)
    bottom = jnp.where(core == 0, corner_other, corner)
    low, inv = factor(top, bottom)
    slots = jnp.stack([packed[:, :w], got[0][:, :w], got[1][:, :w], got[2][:, :w]])
    slots_other = swap(slots)
    b0 = jnp.where(core == 0, slots, slots_other)
    b1 = jnp.where(core == 0, slots_other, slots)
    info = jnp.stack([y, x, row, z]).astype(jnp.int32)
    return update(info, kernel, first, second, b0, b1, low, inv)


def solution(mesh):
    return jax.shard_map(
        local,
        mesh=mesh,
        in_specs=(P("row", "col"),),
        out_specs=P("row", "col"),
        check_vma=False,
    )
```

```python
import jax
import jax.numpy as jnp
from jax import lax
from jax.experimental import pallas as pl
from jax.experimental.pallas import tpu as pltpu
from jax.sharding import PartitionSpec as P

NB = 128
HIGHEST = lax.Precision.HIGHEST
F32 = jnp.float32
BF16 = jnp.bfloat16


def bc(v): return jnp.broadcast_to(v,(8,NB))
def eliminate4(full):
    eye=(lax.broadcasted_iota(jnp.int32,(NB,NB),0)==lax.broadcasted_iota(jnp.int32,(NB,NB),1)).astype(F32)
    G=NB//8
    A=[full[8*g:8*g+8,:] for g in range(G)]
    I=[eye[8*g:8*g+8,:] for g in range(G)]
    sub=lax.broadcasted_iota(jnp.int32,(8,NB),0)
    lane=lax.broadcasted_iota(jnp.int32,(8,NB),1)
    outU=[];outW=[]
    for k in range(0,NB,4):
        g0,s=divmod(k,8)
        C=[bc(A[g0][:,k+a:k+a+1]) for a in range(4)]
        D=[[bc(C[a][s+b:s+b+1,:]) if b<=a else None for b in range(4)] for a in range(4)]
        ra=[bc(A[g0][s+b:s+b+1,:]) for b in range(4)]
        ri=[bc(I[g0][s+b:s+b+1,:]) for b in range(4)]
        p00,p10,p11=D[0][0],D[1][0],D[1][1]
        ip=1.0/(p00*p11-p10*p10)
        i00,i10,i11=p11*ip,-p10*ip,p00*ip
        q20,q21,q30,q31=D[2][0],D[2][1],D[3][0],D[3][1]
        t02=i00*q20+i10*q21; t12=i10*q20+i11*q21
        t03=i00*q30+i10*q31; t13=i10*q30+i11*q31
        s22=D[2][2]-(q20*t02+q21*t12)
        s32=D[3][2]-(q30*t02+q31*t12)
        s33=D[3][3]-(q30*t03+q31*t13)
        isd=1.0/(s22*s33-s32*s32)
        j22,j32,j33=s33*isd,-s32*isd,s22*isd
        def solve(r):
            y2=r[2]-(t02*r[0]+t12*r[1])
            y3=r[3]-(t03*r[0]+t13*r[1])
            x2=j22*y2+j32*y3; x3=j32*y2+j33*y3
            x0=(i00*r[0]+i10*r[1])-(t02*x2+t03*x3)
            x1=(i10*r[0]+i11*r[1])-(t12*x2+t13*x3)
            return [x0,x1,x2,x3],y2,y3
        xa,ya2,ya3=solve(ra)
        xi,yi2,yi3=solve(ri)
        for g in range(g0,G):
            if g==g0:
                if s==4: continue
                c=[jnp.where(sub>=4,v,0.0) for v in C]
            else:
                c=[bc(A[g][:,k+a:k+a+1]) for a in range(4)]
            A[g]=A[g]-((c[0]*xa[0]+c[1]*xa[1])+(c[2]*xa[2]+c[3]*xa[3]))
            I[g]=I[g]-((c[0]*xi[0]+c[1]*xi[1])+(c[2]*xi[2]+c[3]*xi[3]))
        def rsq(x):
            r=lax.rsqrt(x); return r*(1.5-0.5*x*r*r)
        def norm2(d00,d10,d11,r0,r1):
            rs0=rsq(d00); l10=d10*rs0; e=d11-l10*l10; rs1=rsq(e)
            return lambda r0,r1:(r0*rs0,(r1-l10*(r0*rs0))*rs1)
        nP=norm2(p00,p10,p11,None,None); nS=norm2(s22,s32,s33,None,None)
        u=[*nP(ra[0],ra[1]),*nS(ya2,ya3)]
        w=[*nP(ri[0],ri[1]),*nS(yi2,yi3)]
        for b in range(4):
            u[b]=jnp.where(lane>=k+b,u[b],0.0)
        if s==0:
            hu,hw=u,w
        else:
            uu=hu+u; ww=hw+w
            ru=uu[7]; rw=ww[7]
            for b in range(6,-1,-1):
                ru=jnp.where(sub==b,uu[b],ru); rw=jnp.where(sub==b,ww[b],rw)
            outU.append(ru); outW.append(rw)
    return jnp.concatenate(outU,0), jnp.concatenate(outW,0)


def mm(a, b):
    return jnp.dot(a, b, precision=HIGHEST, preferred_element_type=F32)


def mmt(a, b):
    return lax.dot_general(a, b, (((1,), (1,)), ((), ())), precision=HIGHEST, preferred_element_type=F32)


def factor_first(core, mine, other, l_ref, w_ref, s_ref):
    flip = core[0] == 1
    top = jnp.where(flip, other[:, :NB], mine[:, :NB])
    bottom = jnp.where(flip, mine[...], other[...])
    u0, w0 = eliminate4(top)
    l10 = mmt(bottom[:, :NB], w0)
    l_ref[:NB, :] = u0.T
    l_ref[NB:, :] = l10
    w_ref[...] = w0
    s_ref[...] = bottom[:, NB:] - mmt(l10, l10)


def factor_second(l_ref, w0_ref, s_ref, l1_ref, w1_ref):
    u1, w1 = eliminate4(s_ref[...])
    l1_ref[...] = u1.T
    w1_ref[:, :NB] = -mm(mm(w1, l_ref[NB:, :]), w0_ref[...])
    w1_ref[:, NB:] = w1


def sds(*shape):
    return jax.ShapeDtypeStruct(shape, F32)


def vmem(n):
    return [pl.BlockSpec(memory_space=pltpu.VMEM)] * n


def cost(flops, moved):
    return pl.CostEstimate(flops=flops, bytes_accessed=moved, transcendentals=0)


def split(v):
    hi = v.astype(BF16)
    return hi, (v - hi.astype(F32)).astype(BF16)


def update_kernel(info, k_ref, *refs):
    pieces, slots, others = refs[0:8], refs[8:12], refs[12:16]
    l0_ref, w0_ref, l1_ref, w1_ref, out_ref, asm, bs, rows, rhi, rlo = refs[16:]
    step = pl.program_id(0)
    y, x, d, z = info[0], info[1], info[2], info[3]
    core = d % 2
    w = bs.shape[1] // 4
    dot = lambda a, b: jnp.dot(a, b, preferred_element_type=F32)

    @pl.when(step == 0)
    def _():
        for ref, shift in zip(pieces, (0, 4, 7, 3, 1, 5, 2, 6)):
            c = (z + shift) % 8
            asm[c % 2 * 4 + c // 2] = ref[...]
        q = asm.shape[1]
        first = asm[0:4].reshape(4 * q, NB)
        second = asm[4:8].reshape(4 * q, NB)
        w0 = w0_ref[...]
        pan0 = mmt(first, w0)
        pan1 = mmt(first, w1_ref[:, :NB]) + mmt(second, w1_ref[:, NB:])
        rows[:, :NB] = pan0
        rows[:, NB:] = pan1
        for i, v in enumerate((pan0, pan1)):
            hi, lo = split(v)
            rhi[:, i * NB : (i + 1) * NB] = hi
            rlo[:, i * NB : (i + 1) * NB] = lo

        @pl.when(d == 0)
        def _():
            rows[:NB, :NB] = l0_ref[:NB, :]
            rows[:NB, NB:] = jnp.zeros((NB, NB), F32)

        @pl.when(d == 1)
        def _():
            rows[:NB, NB:] = l1_ref[...]

        for s in range(4):
            for group, place_p, block in ((slots, jnp.where(core == 0, y, x), core), (others, jnp.where(core == 0, x, y), 1 - core)):
                n = (place_p - s + 4) % 4
                bs[pl.ds(pl.multiple_of(block * NB, NB), NB), pl.ds(pl.multiple_of(n * w, NB), w)] = group[s][...]

    width = out_ref.shape[1]
    here = pl.ds(pl.multiple_of(step * width, NB), width)
    b0 = bs[:NB, here]
    b1 = bs[NB:, here]
    c0 = mm(w0_ref[...], b0)
    c1 = mm(w1_ref[:, :NB], b0) + mm(w1_ref[:, NB:], b1)
    chi, clo = split(jnp.concatenate([c0, c1], 0))
    prod = dot(rhi[...], chi) + (dot(rlo[...], chi) + dot(rhi[...], clo))
    out_ref[...] = k_ref[...] - prod

    @pl.when(d < 2)
    def _():
        out_ref[:NB, :] = jnp.zeros((NB, width), F32)

    @pl.when((step == 0) & (z == 0))
    def _():
        out_ref[:, :NB] = rows[:, :NB]

    @pl.when((step == 0) & (z == 1))
    def _():
        out_ref[:, :NB] = rows[:, NB:]


def update(info, kernel, pieces, slots, others, l0, w0, l1, w1):
    r, c = kernel.shape
    w = c // STEPS
    operands = [*pieces, *slots, *others, l0, w0, l1, w1]
    whole = [pl.BlockSpec(v.shape, lambda n, s: (0, 0)) for v in operands]
    return pl.pallas_call(
        update_kernel,
        out_shape=sds(r, c),
        grid_spec=pltpu.PrefetchScalarGridSpec(
            num_scalar_prefetch=1,
            grid=(STEPS,),
            in_specs=[pl.BlockSpec((r, w), lambda n, s: (0, n)), *whole],
            out_specs=pl.BlockSpec((r, w), lambda n, s: (0, n)),
            scratch_shapes=[
                pltpu.VMEM((8, r // 4, NB), F32),
                pltpu.VMEM((2 * NB, c), F32),
                pltpu.VMEM((r, 2 * NB), F32),
                pltpu.VMEM((r, 2 * NB), BF16),
                pltpu.VMEM((r, 2 * NB), BF16),
            ],
        ),
        compiler_params=pltpu.CompilerParams(
            dimension_semantics=("arbitrary",), vmem_limit_bytes=40 * 1024 * 1024
        ),
        cost_estimate=cost(5_000_000_000, 18_000_000),
        name="update",
    )(info, kernel, *operands)


STEPS = 5


def place(core, p, q):
    return p * 8 + q * 2 if core == 0 else q * 8 + p * 2 + 1


BOTH = ("row", "col")


def local(kernel):
    row = lax.axis_index("row")
    z = lax.axis_index("col")
    y, x, core = row // 8, row // 2 % 4, row % 2
    p = jnp.where(core == 0, y, x)
    q = jnp.where(core == 0, x, y)
    info = jnp.stack([y, x, row, z]).astype(jnp.int32)

    own = kernel[:NB, :NB]
    other = lax.ppermute(own, BOTH, [(r * 8 + a, r * 8 + 1 - a) for r in (0, 1) for a in (0, 1)])
    corner = jnp.where(z == 0, jnp.concatenate([own, other], 1), jnp.concatenate([other, own], 1))
    got = [
        lax.ppermute(corner, BOTH, [(r * 8 + a, r * 8 + b) for r in (0, 1) for a, b in ((0, 8 - n), (1, 1 + n))])
        for n in (3, 2, 1)
    ]
    corner = jnp.where(z < 2, corner, got[0] + got[1] + got[2])
    got = [
        lax.ppermute(corner, "row", [(place(c, 0, 0), place(c, 0, n)) for c in (0, 1)]) for n in (2, 1, 3)
    ]
    corner = jnp.where(q == 0, corner, got[0] + got[1] + got[2])
    got = [
        lax.ppermute(corner, "row", [(place(c, 0, i), place(c, n, i)) for c in (0, 1) for i in range(4)])
        for n in (2, 1, 3)
    ]
    corner = jnp.where(p == 0, corner, got[0] + got[1] + got[2])
    swap = lambda v: lax.ppermute(v, "row", [(i, i ^ 1) for i in range(32)])
    corner_other = swap(corner)

    first = kernel[:, :NB]
    r4 = kernel.shape[0] // 4
    got = [lax.ppermute(first[j * r4 : (j + 1) * r4], "col", [(0, 2 * j), (1, 2 * j + 1)]) for j in (1, 2, 3)]
    piece = jnp.where(z < 2, first[:r4], got[0] + got[1] + got[2])
    shift = lambda v, n: lax.ppermute(v, "col", [((i + n) % 8, i) for i in range(8)])
    piece4 = shift(piece, 4)
    pair = jnp.concatenate([piece, piece4], 0)
    pairs = [pair] + [shift(pair, n) for n in (7, 1, 2)]
    pieces = [v for a in pairs for v in (a[:r4], a[r4:])]

    w = kernel.shape[1] // 4
    quarters = [kernel[:NB, j * w : (j + 1) * w] for j in range(4)]
    got = [
        lax.ppermute(quarters[j], "row", [(place(c, 0, 0), place(c, j, 0)) for c in (0, 1)]) for j in (2, 1, 3)
    ]
    quarter = jnp.where(p == 0, quarters[0], got[0] + got[1] + got[2])
    got = [
        lax.ppermute(quarter, "row", [(place(c, j, 0), place(c, j, n)) for c in (0, 1) for j in range(4)])
        for n in (2, 1, 3)
    ]
    quarter = jnp.where(q == 0, quarter, got[0] + got[1] + got[2])
    slots = [quarter] + [
        lax.ppermute(
            quarter,
            "row",
            [(place(c, j, i), place(c, (j + n) % 4, i)) for c in (0, 1) for j in range(4) for i in range(4)],
        )
        for n in (1, 2, 3)
    ]

    l0, w0, s = pl.pallas_call(
        factor_first,
        in_specs=[pl.BlockSpec(memory_space=pltpu.SMEM)] + vmem(2),
        out_specs=vmem(3),
        out_shape=[sds(2 * NB, NB), sds(NB, NB), sds(NB, NB)],
        cost_estimate=cost(1_000_000_000, 1_000_000),
        name="factor_first",
    )(core.astype(jnp.int32)[None], corner, corner_other)
    s, slots = lax.optimization_barrier((s, slots))
    others = [swap(v) for v in slots]
    l1, w1 = pl.pallas_call(
        factor_second,
        in_specs=vmem(3),
        out_specs=vmem(2),
        out_shape=[sds(NB, NB), sds(NB, 2 * NB)],
        cost_estimate=cost(1_000_000_000, 1_000_000),
        name="factor_second",
    )(l0, w0, s)
    return update(info, kernel, pieces, slots, others, l0, w0, l1, w1)


def solution(mesh):
    return jax.shard_map(
        local,
        mesh=mesh,
        in_specs=(P("row", "col"),),
        out_specs=P("row", "col"),
        check_vma=False,
    )
```

```python
import jax
import jax.numpy as jnp
from jax import lax
from jax.experimental import pallas as pl
from jax.experimental.pallas import tpu as pltpu
from jax.sharding import PartitionSpec as P

NB = 128
HIGHEST = lax.Precision.HIGHEST
F32 = jnp.float32
BF16 = jnp.bfloat16


def bc(v): return jnp.broadcast_to(v,(8,NB))
def eliminate4(full):
    eye=(lax.broadcasted_iota(jnp.int32,(NB,NB),0)==lax.broadcasted_iota(jnp.int32,(NB,NB),1)).astype(F32)
    G=NB//8
    A=[full[8*g:8*g+8,:] for g in range(G)]
    I=[eye[8*g:8*g+8,:] for g in range(G)]
    sub=lax.broadcasted_iota(jnp.int32,(8,NB),0)
    lane=lax.broadcasted_iota(jnp.int32,(8,NB),1)
    outU=[];outW=[]
    for k in range(0,NB,4):
        g0,s=divmod(k,8)
        C=[bc(A[g0][:,k+a:k+a+1]) for a in range(4)]
        D=[[bc(C[a][s+b:s+b+1,:]) if b<=a else None for b in range(4)] for a in range(4)]
        ra=[bc(A[g0][s+b:s+b+1,:]) for b in range(4)]
        ri=[bc(I[g0][s+b:s+b+1,:]) for b in range(4)]
        p00,p10,p11=D[0][0],D[1][0],D[1][1]
        ip=1.0/(p00*p11-p10*p10)
        i00,i10,i11=p11*ip,-p10*ip,p00*ip
        q20,q21,q30,q31=D[2][0],D[2][1],D[3][0],D[3][1]
        t02=i00*q20+i10*q21; t12=i10*q20+i11*q21
        t03=i00*q30+i10*q31; t13=i10*q30+i11*q31
        s22=D[2][2]-(q20*t02+q21*t12)
        s32=D[3][2]-(q30*t02+q31*t12)
        s33=D[3][3]-(q30*t03+q31*t13)
        isd=1.0/(s22*s33-s32*s32)
        j22,j32,j33=s33*isd,-s32*isd,s22*isd
        def solve(r):
            y2=r[2]-(t02*r[0]+t12*r[1])
            y3=r[3]-(t03*r[0]+t13*r[1])
            x2=j22*y2+j32*y3; x3=j32*y2+j33*y3
            x0=(i00*r[0]+i10*r[1])-(t02*x2+t03*x3)
            x1=(i10*r[0]+i11*r[1])-(t12*x2+t13*x3)
            return [x0,x1,x2,x3],y2,y3
        xa,ya2,ya3=solve(ra)
        xi,yi2,yi3=solve(ri)
        for g in range(g0,G):
            if g==g0:
                if s==4: continue
                c=[jnp.where(sub>=4,v,0.0) for v in C]
            else:
                c=[bc(A[g][:,k+a:k+a+1]) for a in range(4)]
            A[g]=A[g]-((c[0]*xa[0]+c[1]*xa[1])+(c[2]*xa[2]+c[3]*xa[3]))
            I[g]=I[g]-((c[0]*xi[0]+c[1]*xi[1])+(c[2]*xi[2]+c[3]*xi[3]))
        def rsq(x):
            r=lax.rsqrt(x); return r*(1.5-0.5*x*r*r)
        def norm2(d00,d10,d11,r0,r1):
            rs0=rsq(d00); l10=d10*rs0; e=d11-l10*l10; rs1=rsq(e)
            return lambda r0,r1:(r0*rs0,(r1-l10*(r0*rs0))*rs1)
        nP=norm2(p00,p10,p11,None,None); nS=norm2(s22,s32,s33,None,None)
        u=[*nP(ra[0],ra[1]),*nS(ya2,ya3)]
        w=[*nP(ri[0],ri[1]),*nS(yi2,yi3)]
        for b in range(4):
            u[b]=jnp.where(lane>=k+b,u[b],0.0)
        if s==0:
            hu,hw=u,w
        else:
            uu=hu+u; ww=hw+w
            ru=uu[7]; rw=ww[7]
            for b in range(6,-1,-1):
                ru=jnp.where(sub==b,uu[b],ru); rw=jnp.where(sub==b,ww[b],rw)
            outU.append(ru); outW.append(rw)
    return jnp.concatenate(outU,0), jnp.concatenate(outW,0)


def mm(a, b):
    return jnp.dot(a, b, precision=HIGHEST, preferred_element_type=F32)


def mmt(a, b):
    return lax.dot_general(a, b, (((1,), (1,)), ((), ())), precision=HIGHEST, preferred_element_type=F32)


def factor_first(core, mine, other, l_ref, w_ref, s_ref):
    flip = core[0] == 1
    top = jnp.where(flip, other[:, :NB], mine[:, :NB])
    bottom = jnp.where(flip, mine[...], other[...])
    u0, w0 = eliminate4(top)
    l10 = mmt(bottom[:, :NB], w0)
    l_ref[:NB, :] = u0.T
    l_ref[NB:, :] = l10
    w_ref[...] = w0
    s_ref[...] = bottom[:, NB:] - mmt(l10, l10)


def factor_second(l_ref, w0_ref, s_ref, l1_ref, w1_ref):
    u1, w1 = eliminate4(s_ref[...])
    l1_ref[...] = u1.T
    w1_ref[:, :NB] = -mm(mm(w1, l_ref[NB:, :]), w0_ref[...])
    w1_ref[:, NB:] = w1


def sds(*shape):
    return jax.ShapeDtypeStruct(shape, F32)


def vmem(n):
    return [pl.BlockSpec(memory_space=pltpu.VMEM)] * n


def cost(flops, moved):
    return pl.CostEstimate(flops=flops, bytes_accessed=moved, transcendentals=0)


def split(v):
    hi = v.astype(BF16)
    return hi, (v - hi.astype(F32)).astype(BF16)


def update_kernel(info, k_ref, *refs):
    halves, slots, others = refs[0:2], refs[2:6], refs[6:10]
    l0_ref, w0_ref, l1_ref, w1_ref, out_ref, asm, bs, rows, rhi, rlo = refs[10:]
    step = pl.program_id(0)
    y, x, d, z = info[0], info[1], info[2], info[3]
    core = d % 2
    w = bs.shape[1] // 4
    dot = lambda a, b: jnp.dot(a, b, preferred_element_type=F32)

    @pl.when(step == 0)
    def _():
        asm[z % 2] = halves[0][...]
        asm[1 - z % 2] = halves[1][...]
        first = asm[0]
        second = asm[1]
        w0 = w0_ref[...]
        pan0 = mmt(first, w0)
        pan1 = mmt(first, w1_ref[:, :NB]) + mmt(second, w1_ref[:, NB:])
        rows[:, :NB] = pan0
        rows[:, NB:] = pan1
        for i, v in enumerate((pan0, pan1)):
            hi, lo = split(v)
            rhi[:, i * NB : (i + 1) * NB] = hi
            rlo[:, i * NB : (i + 1) * NB] = lo

        @pl.when(d == 0)
        def _():
            rows[:NB, :NB] = l0_ref[:NB, :]
            rows[:NB, NB:] = jnp.zeros((NB, NB), F32)

        @pl.when(d == 1)
        def _():
            rows[:NB, NB:] = l1_ref[...]

        for s in range(4):
            for group, place_p, block in ((slots, jnp.where(core == 0, y, x), core), (others, jnp.where(core == 0, x, y), 1 - core)):
                n = (place_p - s + 4) % 4
                bs[pl.ds(pl.multiple_of(block * NB, NB), NB), pl.ds(pl.multiple_of(n * w, NB), w)] = group[s][...]

    width = out_ref.shape[1]
    here = pl.ds(pl.multiple_of(step * width, NB), width)
    b0 = bs[:NB, here]
    b1 = bs[NB:, here]
    c0 = mm(w0_ref[...], b0)
    c1 = mm(w1_ref[:, :NB], b0) + mm(w1_ref[:, NB:], b1)
    chi, clo = split(jnp.concatenate([c0, c1], 0))
    prod = dot(rhi[...], chi) + (dot(rlo[...], chi) + dot(rhi[...], clo))
    out_ref[...] = k_ref[...] - prod

    @pl.when(d < 2)
    def _():
        out_ref[:NB, :] = jnp.zeros((NB, width), F32)

    @pl.when((step == 0) & (z == 0))
    def _():
        out_ref[:, :NB] = rows[:, :NB]

    @pl.when((step == 0) & (z == 1))
    def _():
        out_ref[:, :NB] = rows[:, NB:]


def update(info, kernel, halves, slots, others, l0, w0, l1, w1):
    r, c = kernel.shape
    w = c // STEPS
    operands = [*halves, *slots, *others, l0, w0, l1, w1]
    whole = [pl.BlockSpec(v.shape, lambda n, s: (0, 0)) for v in operands]
    return pl.pallas_call(
        update_kernel,
        out_shape=sds(r, c),
        grid_spec=pltpu.PrefetchScalarGridSpec(
            num_scalar_prefetch=1,
            grid=(STEPS,),
            in_specs=[pl.BlockSpec((r, w), lambda n, s: (0, n)), *whole],
            out_specs=pl.BlockSpec((r, w), lambda n, s: (0, n)),
            scratch_shapes=[
                pltpu.VMEM((2, r, NB), F32),
                pltpu.VMEM((2 * NB, c), F32),
                pltpu.VMEM((r, 2 * NB), F32),
                pltpu.VMEM((r, 2 * NB), BF16),
                pltpu.VMEM((r, 2 * NB), BF16),
            ],
        ),
        compiler_params=pltpu.CompilerParams(
            dimension_semantics=("arbitrary",), vmem_limit_bytes=28 * 1024 * 1024
        ),
        cost_estimate=cost(5_000_000_000, 18_000_000),
        name="update",
    )(info, kernel, *operands)


STEPS = 5


def place(core, p, q):
    return p * 8 + q * 2 if core == 0 else q * 8 + p * 2 + 1


BOTH = ("row", "col")


def whole_permute(v, axis, pairs):
    stride, size = (8, 256) if axis == BOTH else (1, 32)
    to = dict(pairs)
    back = {b: a for a, b in pairs}
    for b in list(back):
        if b not in to:
            a = b
            while a in back:
                a = back[a]
            to[b] = a
    real = dict(pairs)
    for i in range(size):
        j = i ^ stride
        if i in to:
            continue
        if j not in to:
            to[i], to[j] = j, i
        elif j not in real:
            to[i], to[j] = to[j], i
        else:
            k = next(a for a, b in to.items() if b == j)
            assert k not in real
            to[i], to[k] = j, i
    return lax.ppermute(v, axis, sorted(to.items()))


def pick(i, *values):
    out = values[-1]
    for n in range(len(values) - 2, -1, -1):
        out = jnp.where(i == n, values[n], out)
    return out


def local(kernel):
    row = lax.axis_index("row")
    z = lax.axis_index("col")
    y, x, core = row // 8, row // 2 % 4, row % 2
    p = jnp.where(core == 0, y, x)
    q = jnp.where(core == 0, x, y)
    info = jnp.stack([y, x, row, z]).astype(jnp.int32)

    own = kernel[:NB, :NB]
    other = whole_permute(own, BOTH, [(r * 8 + a, r * 8 + 1 - a) for r in (0, 1) for a in (0, 1)])
    corner = jnp.where(z == 0, jnp.concatenate([own, other], 1), jnp.concatenate([other, own], 1))
    got = [
        whole_permute(corner, BOTH, [(r * 8 + a, r * 8 + b) for r in (0, 1) for a, b in ((0, 8 - n), (1, 1 + n))])
        for n in (3, 2, 1)
    ]
    corner = pick(z, corner, corner, got[2], got[1], got[0], got[0], got[1], got[2])
    first = kernel[:, :NB]
    corner, first = lax.optimization_barrier((corner, first))
    got = [
        whole_permute(corner, "row", [(place(c, 0, 0), place(c, 0, n)) for c in (0, 1)]) for n in (2, 1, 3)
    ]
    corner = pick(q, corner, got[1], got[0], got[2])
    got = [
        whole_permute(corner, "row", [(place(c, 0, i), place(c, n, i)) for c in (0, 1) for i in range(4)])
        for n in (2, 1, 3)
    ]
    corner = pick(p, corner, got[1], got[0], got[2])
    swap = lambda v: lax.ppermute(v, "row", [(i, i ^ 1) for i in range(32)])
    corner_other = swap(corner)

    mesh_line = lambda pairs: [(r * 8 + a, r * 8 + b) for r in range(32) for a, b in pairs]
    far = whole_permute(first, BOTH, mesh_line(((0, 4), (1, 5))))
    half = jnp.where((z == 4) | (z == 5), far, first)
    near = whole_permute(half, BOTH, mesh_line(((0, 2), (1, 3), (4, 6), (5, 7))))
    half = jnp.where((z % 4) < 2, half, near)
    half_other = whole_permute(half, BOTH, mesh_line([(i, i ^ 1) for i in range(8)]))

    w = kernel.shape[1] // 4
    quarters = [kernel[:NB, j * w : (j + 1) * w] for j in range(4)]
    got = [
        whole_permute(quarters[j], "row", [(place(c, 0, 0), place(c, j, 0)) for c in (0, 1)]) for j in (2, 1, 3)
    ]
    quarter = pick(p, quarters[0], got[1], got[0], got[2])
    got = [
        whole_permute(quarter, "row", [(place(c, j, 0), place(c, j, n)) for c in (0, 1) for j in range(4)])
        for n in (2, 1, 3)
    ]
    quarter = pick(q, quarter, got[1], got[0], got[2])
    slots = [quarter] + [
        lax.ppermute(
            quarter,
            "row",
            [(place(c, j, i), place(c, (j + n) % 4, i)) for c in (0, 1) for j in range(4) for i in range(4)],
        )
        for n in (1, 2, 3)
    ]

    l0, w0, s = pl.pallas_call(
        factor_first,
        in_specs=[pl.BlockSpec(memory_space=pltpu.SMEM)] + vmem(2),
        out_specs=vmem(3),
        out_shape=[sds(2 * NB, NB), sds(NB, NB), sds(NB, NB)],
        compiler_params=pltpu.CompilerParams(vmem_limit_bytes=4 * 1024 * 1024),
        cost_estimate=cost(1_000_000_000, 1_000_000),
        name="factor_first",
    )(core.astype(jnp.int32)[None], corner, corner_other)
    s, slots = lax.optimization_barrier((s, slots))
    others = [swap(v) for v in slots]
    l1, w1 = pl.pallas_call(
        factor_second,
        in_specs=vmem(3),
        out_specs=vmem(2),
        out_shape=[sds(NB, NB), sds(NB, 2 * NB)],
        compiler_params=pltpu.CompilerParams(vmem_limit_bytes=4 * 1024 * 1024),
        cost_estimate=cost(1_000_000_000, 1_000_000),
        name="factor_second",
    )(l0, w0, s)
    return update(info, kernel, [half, half_other], slots, others, l0, w0, l1, w1)


def solution(mesh):
    return jax.shard_map(
        local,
        mesh=mesh,
        in_specs=(P("row", "col"),),
        out_specs=P("row", "col"),
        check_vma=False,
    )
```

```python
import jax
import jax.numpy as jnp
from jax import lax
from jax.experimental import pallas as pl
from jax.experimental.pallas import tpu as pltpu
from jax.sharding import PartitionSpec as P

NB = 128
HIGHEST = lax.Precision.HIGHEST
F32 = jnp.float32
BF16 = jnp.bfloat16


def bc(v):
    return jnp.broadcast_to(v, (8, NB))


def identity():
    r=lax.broadcasted_iota(jnp.int32,(NB,NB),0)
    c=lax.broadcasted_iota(jnp.int32,(NB,NB),1)
    return (r==c).astype(F32)


def eliminate(left,right,lo,hi):
    G=NB//8
    A=[left[8*g:8*g+8,:] for g in range(G)]
    I=[right[8*g:8*g+8,:] for g in range(G)]
    sub=lax.broadcasted_iota(jnp.int32,(8,NB),0)
    lane=lax.broadcasted_iota(jnp.int32,(8,NB),1)
    outU=[];outW=[]
    def rsq(x):
        r=lax.rsqrt(x); return r*(1.5-0.5*x*r*r)
    for g0 in range(lo,hi):
        k=8*g0
        C=[bc(A[g0][:,k+a:k+a+1]) for a in range(8)]
        D=[[bc(C[a][b:b+1,:]) for b in range(a+1)] for a in range(8)]
        T=[[None]*8 for _ in range(8)]
        inv=[]
        for j in range(0,8,2):
            p00,p10,p11=D[j][j],D[j+1][j],D[j+1][j+1]
            ip=1.0/(p00*p11-p10*p10)
            i00,i10,i11=p11*ip,-p10*ip,p00*ip
            inv.append((i00,i10,i11,p00,p10,p11))
            for r in range(j+2,8):
                T[r][j]=i00*D[r][j]+i10*D[r][j+1]
                T[r][j+1]=i10*D[r][j]+i11*D[r][j+1]
            for r in range(j+2,8):
                for c in range(j+2,r+1):
                    D[r][c]=D[r][c]-(D[r][j]*T[c][j]+D[r][j+1]*T[c][j+1])
        def solve(x):
            y=[bc(x[b:b+1,:]) for b in range(8)]
            for j in range(0,8,2):
                for r in range(j+2,8):
                    y[r]=y[r]-(T[r][j]*y[j]+T[r][j+1]*y[j+1])
            X=[None]*8
            for j in (6,4,2,0):
                i00,i10,i11=inv[j//2][:3]
                a=i00*y[j]+i10*y[j+1]; b=i10*y[j]+i11*y[j+1]
                for r in range(j+2,8):
                    a=a-T[r][j]*X[r]; b=b-T[r][j+1]*X[r]
                X[j],X[j+1]=a,b
            return y,X
        ya,xa=solve(A[g0])
        yi,xi=solve(I[g0])
        for g in range(g0+1,G):
            c=[bc(A[g][:,k+a:k+a+1]) for a in range(8)]
            def acc(x):
                t=[c[a]*x[a] for a in range(8)]
                return ((t[0]+t[1])+(t[2]+t[3]))+((t[4]+t[5])+(t[6]+t[7]))
            A[g]=A[g]-acc(xa)
            I[g]=I[g]-acc(xi)
        u=[];w=[]
        for j in range(0,8,2):
            p00,p10,p11=inv[j//2][3:]
            rs0=rsq(p00); l10=p10*rs0; rs1=rsq(p11-l10*l10)
            for y,o in ((ya,u),(yi,w)):
                o.append(y[j]*rs0); o.append((y[j+1]-l10*o[-1])*rs1)
        ru,rw=u[7],w[7]
        for b in range(6,-1,-1):
            ru=jnp.where(sub==b,u[b],ru); rw=jnp.where(sub==b,w[b],rw)
        outU.append(jnp.where(lane>=sub+k,ru,0.0)); outW.append(rw)
    rest = (jnp.concatenate(A[hi:],0),jnp.concatenate(I[hi:],0)) if hi<G else None
    return jnp.concatenate(outU,0), jnp.concatenate(outW,0), rest


def mm(a, b):
    return jnp.dot(a, b, precision=HIGHEST, preferred_element_type=F32)


def mmt(a, b):
    return lax.dot_general(a, b, (((1,), (1,)), ((), ())), precision=HIGHEST, preferred_element_type=F32)


def factor_first(core, mine, other, l_ref, w_ref, s_ref):
    flip = core[0] == 1
    top = jnp.where(flip, other[:, :NB], mine[:, :NB])
    bottom = jnp.where(flip, mine[...], other[...])
    u0, w0, _ = eliminate(top, identity(), 0, NB // 8)
    l10 = mmt(bottom[:, :NB], w0)
    l_ref[:NB, :] = u0.T
    l_ref[NB:, :] = l10
    w_ref[...] = w0
    s_ref[...] = bottom[:, NB:] - mmt(l10, l10)


def factor_second(s_ref, a_ref, i_ref):
    u, w, (a, i) = eliminate(s_ref[...], identity(), 0, NB // 16)
    a_ref[: NB // 2] = u
    a_ref[NB // 2 :] = a
    i_ref[: NB // 2] = w
    i_ref[NB // 2 :] = i


def factor_third(a_ref, i_ref, l_ref, w0_ref, l1_ref, w1_ref):
    u, w, _ = eliminate(a_ref[...], i_ref[...], NB // 16, NB // 8)
    u = jnp.concatenate([a_ref[: NB // 2], u], 0)
    w = jnp.concatenate([i_ref[: NB // 2], w], 0)
    l1_ref[...] = u.T
    w1_ref[:, :NB] = -mm(mm(w, l_ref[NB:, :]), w0_ref[...])
    w1_ref[:, NB:] = w


def sds(*shape):
    return jax.ShapeDtypeStruct(shape, F32)


def vmem(n):
    return [pl.BlockSpec(memory_space=pltpu.VMEM)] * n


def cost(flops, moved):
    return pl.CostEstimate(flops=flops, bytes_accessed=moved, transcendentals=0)


def split(v):
    hi = v.astype(BF16)
    return hi, (v - hi.astype(F32)).astype(BF16)


def update_kernel(info, k_ref, h0, h1, s0, s1, s2, s3, o0, o1, o2, o3, l0_ref, w0_ref, l1_ref, w1_ref, out_ref, bs, wf, rows, r3, c3, buf, sems):
    y, x, d, z = info[0], info[1], info[2], info[3]
    core = d % 2
    w = bs.shape[1] // 4
    dot = lambda a, b: jnp.dot(a, b, preferred_element_type=F32)

    for group, p, block in (
        ((s0, s1, s2, s3), jnp.where(core == 0, y, x), core),
        ((o0, o1, o2, o3), jnp.where(core == 0, x, y), 1 - core),
    ):
        for s in range(4):
            n = (p - s + 4) % 4
            bs[pl.ds(pl.multiple_of(block * NB, NB), NB), pl.ds(pl.multiple_of(n * w, NB), w)] = group[s][...]

    wf[:NB, :NB] = w0_ref[...]
    wf[:NB, NB:] = jnp.zeros((NB, NB), F32)
    wf[NB:, :] = w1_ref[...]
    even = z % 2 == 0
    first = jnp.where(even, h0[...], h1[...])
    second = jnp.where(even, h1[...], h0[...])
    pan = mmt(jnp.concatenate([first, second], 1), wf[...])
    rows[...] = pan
    hi, lo = split(pan)
    r3[:, : 2 * NB] = hi
    r3[:, 2 * NB : 4 * NB] = lo
    r3[:, 4 * NB :] = hi

    @pl.when(d == 0)
    def _():
        rows[:NB, :NB] = l0_ref[:NB, :]
        rows[:NB, NB:] = jnp.zeros((NB, NB), F32)

    @pl.when(d == 1)
    def _():
        rows[:NB, NB:] = l1_ref[...]

    whi, wlo = split(wf[...])
    w3 = jnp.concatenate([whi, wlo, whi], 1)
    r, c = buf.shape
    width = c // STEPS
    copies = []

    for n in range(5):
        here = slice(n * c // 5, (n + 1) * c // 5)
        bhi, blo = split(bs[:, here])
        chi, clo = split(dot(w3, jnp.concatenate([bhi, bhi, blo], 0)))
        c3[: 2 * NB, here] = chi
        c3[2 * NB : 4 * NB, here] = chi
        c3[4 * NB :, here] = clo

    for n in range(STEPS):
        here = slice(n * width, (n + 1) * width)
        buf[:, here] = k_ref[:, here] - dot(r3[...], c3[:, here])

        @pl.when(d < 2)
        def _():
            buf[:NB, here] = jnp.zeros((NB, width), F32)

        if n == 0:

            @pl.when(z == 0)
            def _():
                buf[:, :NB] = rows[:, :NB]

            @pl.when(z == 1)
            def _():
                buf[:, :NB] = rows[:, NB:]

        copy = pltpu.make_async_copy(buf.at[:, here], out_ref.at[:, here], sems.at[n])
        copy.start()
        copies.append(copy)
    for copy in copies:
        copy.wait()


def update(info, kernel, halves, slots, others, l0, w0, l1, w1):
    r, c = kernel.shape
    operands = [kernel, *halves, *slots, *others, l0, w0, l1, w1]
    return pl.pallas_call(
        update_kernel,
        out_shape=sds(r, c),
        in_specs=[pl.BlockSpec(memory_space=pltpu.SMEM)] + vmem(len(operands)),
        out_specs=pl.BlockSpec(memory_space=pl.ANY),
        scratch_shapes=[
            pltpu.VMEM((2 * NB, c), F32),
            pltpu.VMEM((2 * NB, 2 * NB), F32),
            pltpu.VMEM((r, 2 * NB), F32),
            pltpu.VMEM((r, 6 * NB), BF16),
            pltpu.VMEM((6 * NB, c), BF16),
            pltpu.VMEM((r, c), F32),
            pltpu.SemaphoreType.DMA((STEPS,)),
        ],
        compiler_params=pltpu.CompilerParams(vmem_limit_bytes=32 * 1024 * 1024),
        cost_estimate=cost(5_000_000_000, 18_000_000),
        name="update",
    )(info, *operands)


STEPS = 5


def place(core, p, q):
    return p * 8 + q * 2 if core == 0 else q * 8 + p * 2 + 1


BOTH = ("row", "col")


def whole_permute(v, axis, pairs):
    stride, size = (8, 256) if axis == BOTH else (1, 32)
    to = dict(pairs)
    back = {b: a for a, b in pairs}
    for b in list(back):
        if b not in to:
            a = b
            while a in back:
                a = back[a]
            to[b] = a
    real = dict(pairs)
    for i in range(size):
        j = i ^ stride
        if i in to:
            continue
        if j not in to:
            to[i], to[j] = j, i
        elif j not in real:
            to[i], to[j] = to[j], i
        else:
            k = next(a for a, b in to.items() if b == j)
            assert k not in real
            to[i], to[k] = j, i
    return lax.ppermute(v, axis, sorted(to.items()))


def pick(i, *values):
    out = values[-1]
    for n in range(len(values) - 2, -1, -1):
        out = jnp.where(i == n, values[n], out)
    return out


def local(kernel):
    row = lax.axis_index("row")
    z = lax.axis_index("col")
    y, x, core = row // 8, row // 2 % 4, row % 2
    p = jnp.where(core == 0, y, x)
    q = jnp.where(core == 0, x, y)
    info = jnp.stack([y, x, row, z]).astype(jnp.int32)

    swap = lambda v: lax.ppermute(v, "row", [(i, i ^ 1) for i in range(32)])
    in_line = lambda pairs: [(r * 8 + a, r * 8 + b) for r in (0, 1) for a, b in pairs]
    in_lines = lambda pairs: [(r * 8 + a, r * 8 + b) for r in range(32) for a, b in pairs]
    w = kernel.shape[1] // 4

    own = kernel[:NB, :NB]
    quarters = [kernel[:NB, j * w : (j + 1) * w] for j in range(4)]
    other = whole_permute(own, BOTH, in_line(((0, 1), (1, 0))))
    scattered = [
        whole_permute(quarters[j], "row", [(place(c, 0, 0), place(c, j, 0)) for c in (0, 1)]) for j in (2, 1, 3)
    ]
    corner = jnp.where(z == 0, jnp.concatenate([own, other], 1), jnp.concatenate([other, own], 1))
    two = whole_permute(corner, BOTH, in_line(((0, 6), (1, 3))))
    one = whole_permute(corner, BOTH, in_line(((0, 7), (1, 2))))
    corner = pick(z, corner, corner, one, two, two, two, two, one)
    quarter = pick(p, quarters[0], scattered[1], scattered[0], scattered[2])
    first = kernel[:, :NB]
    corner, quarter, first = lax.optimization_barrier((corner, quarter, first))
    last = whole_permute(corner, BOTH, in_line(((6, 5), (3, 4))))
    corner = jnp.where((z == 4) | (z == 5), last, corner)

    far = whole_permute(first, BOTH, in_lines(((0, 4), (1, 5))))

    spread = [
        whole_permute(quarter, "row", [(place(c, j, 0), place(c, j, n)) for c in (0, 1) for j in range(4)])
        for n in (2, 1, 3)
    ]
    got = [whole_permute(corner, "row", [(place(c, 0, 0), place(c, 0, n)) for c in (0, 1)]) for n in (2, 1, 3)]
    corner = pick(q, corner, got[1], got[0], got[2])
    got = [
        whole_permute(corner, "row", [(place(c, 0, i), place(c, n, i)) for c in (0, 1) for i in range(4)])
        for n in (2, 1, 3)
    ]
    corner = pick(p, corner, got[1], got[0], got[2])
    quarter = pick(q, quarter, spread[1], spread[0], spread[2])
    half = jnp.where((z == 4) | (z == 5), far, first)
    corner, quarter, half = lax.optimization_barrier((corner, quarter, half))

    corner_other = swap(corner)
    slots = [
        lax.ppermute(
            quarter,
            "row",
            [(place(c, j, i), place(c, (j + n) % 4, i)) for c in (0, 1) for j in range(4) for i in range(4)],
        )
        for n in (1, 2, 3)
    ]
    near = whole_permute(half, BOTH, in_lines(((0, 2), (1, 3), (4, 6), (5, 7))))
    l0, w0, s = kernel_call(factor_first, "factor_first", [(2 * NB, NB), (NB, NB), (NB, NB)], 1)(
        core.astype(jnp.int32)[None], corner, corner_other
    )
    half = jnp.where((z % 4) < 2, half, near)
    s, half = lax.optimization_barrier((s, half))
    half_other = whole_permute(half, BOTH, in_lines([(i, i ^ 1) for i in range(8)]))
    left, right = kernel_call(factor_second, "factor_second", [(NB, NB), (NB, NB)])(s)
    left, right, quarter, slots = lax.optimization_barrier((left, right, quarter, slots))
    slots = [quarter, *slots]
    others = [swap(v) for v in slots]
    l1, w1 = kernel_call(factor_third, "factor_third", [(NB, NB), (NB, 2 * NB)])(left, right, l0, w0)
    return update(info, kernel, [half, half_other], slots, others, l0, w0, l1, w1)


def kernel_call(body, name, shapes, scalars=0):
    def call(*operands):
        return pl.pallas_call(
            body,
            in_specs=[pl.BlockSpec(memory_space=pltpu.SMEM)] * scalars + vmem(len(operands) - scalars),
            out_specs=vmem(len(shapes)),
            out_shape=[sds(*shape) for shape in shapes],
            compiler_params=pltpu.CompilerParams(vmem_limit_bytes=4 * 1024 * 1024),
            cost_estimate=cost(1_000_000_000, 1_000_000),
            name=name,
        )(*operands)

    return call


def solution(mesh):
    return jax.shard_map(
        local,
        mesh=mesh,
        in_specs=(P("row", "col"),),
        out_specs=P("row", "col"),
        check_vma=False,
    )
```

```python
import jax
import jax.numpy as jnp
from jax import lax
from jax.experimental import pallas as pl
from jax.experimental.pallas import tpu as pltpu
from jax.sharding import PartitionSpec as P

NB = 128
HIGHEST = lax.Precision.HIGHEST
F32 = jnp.float32
BF16 = jnp.bfloat16


def bc(v):
    return jnp.broadcast_to(v, (8, NB))


def identity():
    r=lax.broadcasted_iota(jnp.int32,(NB,NB),0)
    c=lax.broadcasted_iota(jnp.int32,(NB,NB),1)
    return (r==c).astype(F32)


def eliminate(left,right,lo,hi):
    G=NB//8
    A=[left[8*g:8*g+8,:] for g in range(G)]
    I=[right[8*g:8*g+8,:] for g in range(G)]
    sub=lax.broadcasted_iota(jnp.int32,(8,NB),0)
    lane=lax.broadcasted_iota(jnp.int32,(8,NB),1)
    outU=[];outW=[]
    def rsq(x):
        r=lax.rsqrt(x); return r*(1.5-0.5*x*r*r)
    for g0 in range(lo,hi):
        k=8*g0
        C=[bc(A[g0][:,k+a:k+a+1]) for a in range(8)]
        D=[[bc(C[a][b:b+1,:]) for b in range(a+1)] for a in range(8)]
        T=[[None]*8 for _ in range(8)]
        inv=[]
        for j in range(0,8,2):
            p00,p10,p11=D[j][j],D[j+1][j],D[j+1][j+1]
            ip=1.0/(p00*p11-p10*p10)
            i00,i10,i11=p11*ip,-p10*ip,p00*ip
            inv.append((i00,i10,i11,p00,p10,p11))
            for r in range(j+2,8):
                T[r][j]=i00*D[r][j]+i10*D[r][j+1]
                T[r][j+1]=i10*D[r][j]+i11*D[r][j+1]
            for r in range(j+2,8):
                for c in range(j+2,r+1):
                    D[r][c]=D[r][c]-(D[r][j]*T[c][j]+D[r][j+1]*T[c][j+1])
        def solve(x):
            y=[bc(x[b:b+1,:]) for b in range(8)]
            for j in range(0,8,2):
                for r in range(j+2,8):
                    y[r]=y[r]-(T[r][j]*y[j]+T[r][j+1]*y[j+1])
            X=[None]*8
            for j in (6,4,2,0):
                i00,i10,i11=inv[j//2][:3]
                a=i00*y[j]+i10*y[j+1]; b=i10*y[j]+i11*y[j+1]
                for r in range(j+2,8):
                    a=a-T[r][j]*X[r]; b=b-T[r][j+1]*X[r]
                X[j],X[j+1]=a,b
            return y,X
        ya,xa=solve(A[g0])
        yi,xi=solve(I[g0])
        for g in range(g0+1,G):
            c=[bc(A[g][:,k+a:k+a+1]) for a in range(8)]
            def acc(x):
                t=[c[a]*x[a] for a in range(8)]
                return ((t[0]+t[1])+(t[2]+t[3]))+((t[4]+t[5])+(t[6]+t[7]))
            A[g]=A[g]-acc(xa)
            I[g]=I[g]-acc(xi)
        u=[];w=[]
        for j in range(0,8,2):
            p00,p10,p11=inv[j//2][3:]
            rs0=rsq(p00); l10=p10*rs0; rs1=rsq(p11-l10*l10)
            for y,o in ((ya,u),(yi,w)):
                o.append(y[j]*rs0); o.append((y[j+1]-l10*o[-1])*rs1)
        ru,rw=u[7],w[7]
        for b in range(6,-1,-1):
            ru=jnp.where(sub==b,u[b],ru); rw=jnp.where(sub==b,w[b],rw)
        outU.append(jnp.where(lane>=sub+k,ru,0.0)); outW.append(rw)
    rest = (jnp.concatenate(A[hi:],0),jnp.concatenate(I[hi:],0)) if hi<G else None
    return jnp.concatenate(outU,0), jnp.concatenate(outW,0), rest


def mm(a, b):
    return jnp.dot(a, b, precision=HIGHEST, preferred_element_type=F32)


def mmt(a, b):
    return lax.dot_general(a, b, (((1,), (1,)), ((), ())), precision=HIGHEST, preferred_element_type=F32)


def factor_first(core, mine, other, l_ref, w_ref, s_ref):
    flip = core[0] == 1
    top = jnp.where(flip, other[:, :NB], mine[:, :NB])
    bottom = jnp.where(flip, mine[...], other[...])
    u0, w0, _ = eliminate(top, identity(), 0, NB // 8)
    l10 = mmt(bottom[:, :NB], w0)
    l_ref[:NB, :] = u0.T
    l_ref[NB:, :] = l10
    w_ref[...] = w0
    s_ref[...] = bottom[:, NB:] - mmt(l10, l10)


def factor_second(s_ref, a_ref, i_ref):
    u, w, (a, i) = eliminate(s_ref[...], identity(), 0, NB // 16)
    a_ref[: NB // 2] = u
    a_ref[NB // 2 :] = a
    i_ref[: NB // 2] = w
    i_ref[NB // 2 :] = i


def factor_third(a_ref, i_ref, l_ref, w0_ref, l1_ref, w1_ref):
    u, w, _ = eliminate(a_ref[...], i_ref[...], NB // 16, NB // 8)
    u = jnp.concatenate([a_ref[: NB // 2], u], 0)
    w = jnp.concatenate([i_ref[: NB // 2], w], 0)
    l1_ref[...] = u.T
    w1_ref[:, :NB] = -mm(mm(w, l_ref[NB:, :]), w0_ref[...])
    w1_ref[:, NB:] = w


def sds(*shape):
    return jax.ShapeDtypeStruct(shape, F32)


def vmem(n):
    return [pl.BlockSpec(memory_space=pltpu.VMEM)] * n


def cost(flops, moved):
    return pl.CostEstimate(flops=flops, bytes_accessed=moved, transcendentals=0)


def split(v):
    hi = v.astype(BF16)
    return hi, (v - hi.astype(F32)).astype(BF16)


def update_kernel(info, k_ref, h0, h1, s0, s1, s2, s3, o0, o1, o2, o3, l0_ref, w0_ref, l1_ref, w1_ref, out_ref, bs, wf, rows, r3, c3, buf, sems):
    y, x, d, z = info[0], info[1], info[2], info[3]
    core = d % 2
    w = bs.shape[1] // 4
    dot = lambda a, b: jnp.dot(a, b, preferred_element_type=F32)

    for group, p, block in (
        ((s0, s1, s2, s3), jnp.where(core == 0, y, x), core),
        ((o0, o1, o2, o3), jnp.where(core == 0, x, y), 1 - core),
    ):
        for s in range(4):
            n = (p - s + 4) % 4
            bs[pl.ds(pl.multiple_of(block * NB, NB), NB), pl.ds(pl.multiple_of(n * w, NB), w)] = group[s][...]

    wf[:NB, :NB] = w0_ref[...]
    wf[:NB, NB:] = jnp.zeros((NB, NB), F32)
    wf[NB:, :] = w1_ref[...]
    even = z % 2 == 0
    first = jnp.where(even, h0[...], h1[...])
    second = jnp.where(even, h1[...], h0[...])
    pan = mmt(jnp.concatenate([first, second], 1), wf[...])
    rows[...] = pan
    hi, lo = split(pan)
    r3[:, : 2 * NB] = hi
    r3[:, 2 * NB : 4 * NB] = lo
    r3[:, 4 * NB :] = hi

    @pl.when(d == 0)
    def _():
        rows[:NB, :NB] = l0_ref[:NB, :]
        rows[:NB, NB:] = jnp.zeros((NB, NB), F32)

    @pl.when(d == 1)
    def _():
        rows[:NB, NB:] = l1_ref[...]

    whi, wlo = split(wf[...])
    w3 = jnp.concatenate([whi, wlo, whi], 1)
    r, c = buf.shape
    width = c // STEPS
    copies = []

    for n in range(5):
        here = slice(n * c // 5, (n + 1) * c // 5)
        bhi, blo = split(bs[:, here])
        chi, clo = split(dot(w3, jnp.concatenate([bhi, bhi, blo], 0)))
        c3[: 2 * NB, here] = chi
        c3[2 * NB : 4 * NB, here] = chi
        c3[4 * NB :, here] = clo

    for n in range(STEPS):
        here = slice(n * width, (n + 1) * width)
        buf[:, here] = k_ref[:, here] - dot(r3[...], c3[:, here])

        @pl.when(d < 2)
        def _():
            buf[:NB, here] = jnp.zeros((NB, width), F32)

        if n == 0:

            @pl.when(z == 0)
            def _():
                buf[:, :NB] = rows[:, :NB]

            @pl.when(z == 1)
            def _():
                buf[:, :NB] = rows[:, NB:]

        copy = pltpu.make_async_copy(buf.at[:, here], out_ref.at[:, here], sems.at[n])
        copy.start()
        copies.append(copy)
    for copy in copies:
        copy.wait()


def update(info, kernel, halves, slots, others, l0, w0, l1, w1):
    r, c = kernel.shape
    operands = [kernel, *halves, *slots, *others, l0, w0, l1, w1]
    return pl.pallas_call(
        update_kernel,
        out_shape=sds(r, c),
        in_specs=[pl.BlockSpec(memory_space=pltpu.SMEM)] + vmem(len(operands)),
        out_specs=pl.BlockSpec(memory_space=pl.ANY),
        scratch_shapes=[
            pltpu.VMEM((2 * NB, c), F32),
            pltpu.VMEM((2 * NB, 2 * NB), F32),
            pltpu.VMEM((r, 2 * NB), F32),
            pltpu.VMEM((r, 6 * NB), BF16),
            pltpu.VMEM((6 * NB, c), BF16),
            pltpu.VMEM((r, c), F32),
            pltpu.SemaphoreType.DMA((STEPS,)),
        ],
        compiler_params=pltpu.CompilerParams(vmem_limit_bytes=32 * 1024 * 1024),
        cost_estimate=cost(5_000_000_000, 18_000_000),
        name="update",
    )(info, *operands)


STEPS = 5


def place(core, p, q):
    return p * 8 + q * 2 if core == 0 else q * 8 + p * 2 + 1


BOTH = ("row", "col")


def whole_permute(v, axis, pairs):
    stride, size = (8, 256) if axis == BOTH else (1, 32)
    to = dict(pairs)
    back = {b: a for a, b in pairs}
    for b in list(back):
        if b not in to:
            a = b
            while a in back:
                a = back[a]
            to[b] = a
    real = dict(pairs)
    for i in range(size):
        j = i ^ stride
        if i in to:
            continue
        if j not in to:
            to[i], to[j] = j, i
        elif j not in real:
            to[i], to[j] = to[j], i
        else:
            k = next(a for a, b in to.items() if b == j)
            assert k not in real
            to[i], to[k] = j, i
    return lax.ppermute(v, axis, sorted(to.items()))


def pick(i, *values):
    out = values[-1]
    for n in range(len(values) - 2, -1, -1):
        out = jnp.where(i == n, values[n], out)
    return out


def fetch_kernel(k_ref, *refs):
    outs, sems = refs[:-1], refs[-1]
    w = k_ref.shape[1] // 4
    views = [k_ref.at[:NB, :NB], k_ref.at[:, :NB]] + [k_ref.at[:NB, j * w : (j + 1) * w] for j in range(4)]
    copies = [pltpu.make_async_copy(v, o, sems.at[i]) for i, (v, o) in enumerate(zip(views, outs))]
    for copy in copies:
        copy.start()
    for copy in copies:
        copy.wait()


def fetch(kernel):
    r, c = kernel.shape
    shapes = [(NB, NB), (r, NB)] + [(NB, c // 4)] * 4
    return pl.pallas_call(
        fetch_kernel,
        in_specs=[pl.BlockSpec(memory_space=pl.ANY)],
        out_specs=vmem(len(shapes)),
        out_shape=[sds(*shape) for shape in shapes],
        scratch_shapes=[pltpu.SemaphoreType.DMA((len(shapes),))],
        compiler_params=pltpu.CompilerParams(vmem_limit_bytes=56 * 1024 * 1024),
        name="fetch",
    )(kernel)


def local(kernel):
    row = lax.axis_index("row")
    z = lax.axis_index("col")
    y, x, core = row // 8, row // 2 % 4, row % 2
    p = jnp.where(core == 0, y, x)
    q = jnp.where(core == 0, x, y)
    info = jnp.stack([y, x, row, z]).astype(jnp.int32)

    swap = lambda v: lax.ppermute(v, "row", [(i, i ^ 1) for i in range(32)])
    in_line = lambda pairs: [(r * 8 + a, r * 8 + b) for r in (0, 1) for a, b in pairs]
    in_lines = lambda pairs: [(r * 8 + a, r * 8 + b) for r in range(32) for a, b in pairs]
    w = kernel.shape[1] // 4

    own, first, *quarters = fetch(kernel)

    other = whole_permute(own, BOTH, in_line(((0, 1), (1, 0))))
    scattered = [
        whole_permute(quarters[j], "row", [(place(c, 0, 0), place(c, j, 0)) for c in (0, 1)]) for j in (2, 1, 3)
    ]
    far = whole_permute(first, BOTH, in_lines(((0, 4), (1, 5))))
    other, scattered = lax.optimization_barrier((other, scattered))

    corner = jnp.where(z == 0, jnp.concatenate([own, other], 1), jnp.concatenate([other, own], 1))
    got = [whole_permute(corner, BOTH, in_line(((0, 8 - n), (1, 1 + n)))) for n in (3, 2, 1)]
    corner = pick(z, corner, corner, got[2], got[1], got[0], got[0], got[1], got[2])
    quarter = pick(p, quarters[0], scattered[1], scattered[0], scattered[2])
    packed = jnp.concatenate([quarter, corner], 1)
    half = jnp.where((z == 4) | (z == 5), far, first)
    packed, half = lax.optimization_barrier((packed, half))

    got = [
        whole_permute(packed, "row", [(place(c, j, 0), place(c, j, n)) for c in (0, 1) for j in range(4)])
        for n in (2, 1, 3)
    ]
    near = whole_permute(half, BOTH, in_lines(((0, 2), (1, 3), (4, 6), (5, 7))))
    packed = pick(q, packed, got[1], got[0], got[2])
    half = jnp.where((z % 4) < 2, half, near)
    packed, half = lax.optimization_barrier((packed, half))
    corner, quarter = packed[:, w:], packed[:, :w]

    got = [
        whole_permute(corner, "row", [(place(c, 0, i), place(c, n, i)) for c in (0, 1) for i in range(4)])
        for n in (2, 1, 3)
    ]
    corner = pick(p, corner, got[1], got[0], got[2])
    corner_other = swap(corner)
    slots = [
        lax.ppermute(
            quarter,
            "row",
            [(place(c, j, i), place(c, (j + n) % 4, i)) for c in (0, 1) for j in range(4) for i in range(4)],
        )
        for n in (1, 2, 3)
    ]
    half_other = whole_permute(half, BOTH, in_lines([(i, i ^ 1) for i in range(8)]))
    l0, w0, s = kernel_call(factor_first, "factor_first", [(2 * NB, NB), (NB, NB), (NB, NB)], 1)(
        core.astype(jnp.int32)[None], corner, corner_other
    )
    left, right = kernel_call(factor_second, "factor_second", [(NB, NB), (NB, NB)])(s)
    left, right, quarter, slots = lax.optimization_barrier((left, right, quarter, slots))
    slots = [quarter, *slots]
    others = [swap(v) for v in slots]
    l1, w1 = kernel_call(factor_third, "factor_third", [(NB, NB), (NB, 2 * NB)])(left, right, l0, w0)
    return update(info, kernel, [half, half_other], slots, others, l0, w0, l1, w1)


def kernel_call(body, name, shapes, scalars=0):
    def call(*operands):
        return pl.pallas_call(
            body,
            in_specs=[pl.BlockSpec(memory_space=pltpu.SMEM)] * scalars + vmem(len(operands) - scalars),
            out_specs=vmem(len(shapes)),
            out_shape=[sds(*shape) for shape in shapes],
            compiler_params=pltpu.CompilerParams(vmem_limit_bytes=4 * 1024 * 1024),
            cost_estimate=cost(1_000_000_000, 1_000_000),
            name=name,
        )(*operands)

    return call


def solution(mesh):
    return jax.shard_map(
        local,
        mesh=mesh,
        in_specs=(P("row", "col"),),
        out_specs=P("row", "col"),
        check_vma=False,
    )
```

```python
import jax
import jax.numpy as jnp
from jax import lax
from jax.experimental import pallas as pl
from jax.experimental.pallas import tpu as pltpu
from jax.sharding import PartitionSpec as P

NB = 128
HIGHEST = lax.Precision.HIGHEST
F32 = jnp.float32
BF16 = jnp.bfloat16


def bc(v):
    return jnp.broadcast_to(v, (8, NB))


def identity():
    r=lax.broadcasted_iota(jnp.int32,(NB,NB),0)
    c=lax.broadcasted_iota(jnp.int32,(NB,NB),1)
    return (r==c).astype(F32)


def eliminate(left,right,lo,hi):
    G=NB//8
    A=[left[8*g:8*g+8,:] for g in range(G)]
    I=[right[8*g:8*g+8,:] for g in range(G)]
    sub=lax.broadcasted_iota(jnp.int32,(8,NB),0)
    lane=lax.broadcasted_iota(jnp.int32,(8,NB),1)
    outU=[];outW=[]
    def rsq(x):
        r=lax.rsqrt(x); return r*(1.5-0.5*x*r*r)
    for g0 in range(lo,hi):
        k=8*g0
        C=[bc(A[g0][:,k+a:k+a+1]) for a in range(8)]
        D=[[bc(C[a][b:b+1,:]) for b in range(a+1)] for a in range(8)]
        T=[[None]*8 for _ in range(8)]
        inv=[]
        for j in range(0,8,2):
            p00,p10,p11=D[j][j],D[j+1][j],D[j+1][j+1]
            ip=1.0/(p00*p11-p10*p10)
            i00,i10,i11=p11*ip,-p10*ip,p00*ip
            inv.append((i00,i10,i11,p00,p10,p11))
            for r in range(j+2,8):
                T[r][j]=i00*D[r][j]+i10*D[r][j+1]
                T[r][j+1]=i10*D[r][j]+i11*D[r][j+1]
            for r in range(j+2,8):
                for c in range(j+2,r+1):
                    D[r][c]=D[r][c]-(D[r][j]*T[c][j]+D[r][j+1]*T[c][j+1])
        def solve(x):
            y=[bc(x[b:b+1,:]) for b in range(8)]
            for j in range(0,8,2):
                for r in range(j+2,8):
                    y[r]=y[r]-(T[r][j]*y[j]+T[r][j+1]*y[j+1])
            X=[None]*8
            for j in (6,4,2,0):
                i00,i10,i11=inv[j//2][:3]
                a=i00*y[j]+i10*y[j+1]; b=i10*y[j]+i11*y[j+1]
                for r in range(j+2,8):
                    a=a-T[r][j]*X[r]; b=b-T[r][j+1]*X[r]
                X[j],X[j+1]=a,b
            return y,X
        ya,xa=solve(A[g0])
        yi,xi=solve(I[g0])
        for g in range(g0+1,G):
            c=[bc(A[g][:,k+a:k+a+1]) for a in range(8)]
            def acc(x):
                t=[c[a]*x[a] for a in range(8)]
                return ((t[0]+t[1])+(t[2]+t[3]))+((t[4]+t[5])+(t[6]+t[7]))
            A[g]=A[g]-acc(xa)
            I[g]=I[g]-acc(xi)
        u=[];w=[]
        for j in range(0,8,2):
            p00,p10,p11=inv[j//2][3:]
            rs0=rsq(p00); l10=p10*rs0; rs1=rsq(p11-l10*l10)
            for y,o in ((ya,u),(yi,w)):
                o.append(y[j]*rs0); o.append((y[j+1]-l10*o[-1])*rs1)
        ru,rw=u[7],w[7]
        for b in range(6,-1,-1):
            ru=jnp.where(sub==b,u[b],ru); rw=jnp.where(sub==b,w[b],rw)
        outU.append(jnp.where(lane>=sub+k,ru,0.0)); outW.append(rw)
    rest = (jnp.concatenate(A[hi:],0),jnp.concatenate(I[hi:],0)) if hi<G else None
    return jnp.concatenate(outU,0), jnp.concatenate(outW,0), rest


def mm(a, b):
    return jnp.dot(a, b, precision=HIGHEST, preferred_element_type=F32)


def mmt(a, b):
    return lax.dot_general(a, b, (((1,), (1,)), ((), ())), precision=HIGHEST, preferred_element_type=F32)


def factor_first(core, mine, other, l_ref, w_ref, s_ref):
    flip = core[0] == 1
    top = jnp.where(flip, other[:, :NB], mine[:, :NB])
    bottom = jnp.where(flip, mine[...], other[...])
    u0, w0, _ = eliminate(top, identity(), 0, NB // 8)
    l10 = mmt(bottom[:, :NB], w0)
    l_ref[:NB, :] = u0.T
    l_ref[NB:, :] = l10
    w_ref[...] = w0
    s_ref[...] = bottom[:, NB:] - mmt(l10, l10)


def factor_second(s_ref, l_ref, w0_ref, l1_ref, w1_ref):
    u, w, _ = eliminate(s_ref[...], identity(), 0, NB // 8)
    l1_ref[...] = u.T
    w1_ref[:, :NB] = -mm(mm(w, l_ref[NB:, :]), w0_ref[...])
    w1_ref[:, NB:] = w


def sds(*shape):
    return jax.ShapeDtypeStruct(shape, F32)


def vmem(n):
    return [pl.BlockSpec(memory_space=pltpu.VMEM)] * n


def cost(flops, moved):
    return pl.CostEstimate(flops=flops, bytes_accessed=moved, transcendentals=0)


def split(v):
    hi = v.astype(BF16)
    return hi, (v - hi.astype(F32)).astype(BF16)


def update_kernel(info, k_ref, h0, h1, s0, s1, s2, s3, o0, o1, o2, o3, l0_ref, w0_ref, l1_ref, w1_ref, out_ref, bs, wf, rows, r3, c3, buf, sems):
    y, x, d, z = info[0], info[1], info[2], info[3]
    core = d % 2
    w = bs.shape[1] // 4
    dot = lambda a, b: jnp.dot(a, b, preferred_element_type=F32)

    for group, p, block in (
        ((s0, s1, s2, s3), jnp.where(core == 0, y, x), core),
        ((o0, o1, o2, o3), jnp.where(core == 0, x, y), 1 - core),
    ):
        for s in range(4):
            n = (p - s + 4) % 4
            bs[pl.ds(pl.multiple_of(block * NB, NB), NB), pl.ds(pl.multiple_of(n * w, NB), w)] = group[s][...]

    wf[:NB, :NB] = w0_ref[...]
    wf[:NB, NB:] = jnp.zeros((NB, NB), F32)
    wf[NB:, :] = w1_ref[...]
    even = z % 2 == 0
    first = jnp.where(even, h0[...], h1[...])
    second = jnp.where(even, h1[...], h0[...])
    pan = mmt(jnp.concatenate([first, second], 1), wf[...])
    rows[...] = pan
    hi, lo = split(pan)
    r3[:, : 2 * NB] = hi
    r3[:, 2 * NB : 4 * NB] = lo
    r3[:, 4 * NB :] = hi

    @pl.when(d == 0)
    def _():
        rows[:NB, :NB] = l0_ref[:NB, :]
        rows[:NB, NB:] = jnp.zeros((NB, NB), F32)

    @pl.when(d == 1)
    def _():
        rows[:NB, NB:] = l1_ref[...]

    whi, wlo = split(wf[...])
    w3 = jnp.concatenate([whi, wlo, whi], 1)
    r, c = buf.shape
    width = c // STEPS
    copies = []

    for n in range(5):
        here = slice(n * c // 5, (n + 1) * c // 5)
        bhi, blo = split(bs[:, here])
        chi, clo = split(dot(w3, jnp.concatenate([bhi, bhi, blo], 0)))
        c3[: 2 * NB, here] = chi
        c3[2 * NB : 4 * NB, here] = chi
        c3[4 * NB :, here] = clo

    for n in range(STEPS):
        here = slice(n * width, (n + 1) * width)
        buf[:, here] = k_ref[:, here] - dot(r3[...], c3[:, here])

        @pl.when(d < 2)
        def _():
            buf[:NB, here] = jnp.zeros((NB, width), F32)

        if n == 0:

            @pl.when(z == 0)
            def _():
                buf[:, :NB] = rows[:, :NB]

            @pl.when(z == 1)
            def _():
                buf[:, :NB] = rows[:, NB:]

        copy = pltpu.make_async_copy(buf.at[:, here], out_ref.at[:, here], sems.at[n])
        copy.start()
        copies.append(copy)
    for copy in copies:
        copy.wait()


def update(info, kernel, halves, slots, others, l0, w0, l1, w1):
    r, c = kernel.shape
    operands = [kernel, *halves, *slots, *others, l0, w0, l1, w1]
    return pl.pallas_call(
        update_kernel,
        out_shape=sds(r, c),
        in_specs=[pl.BlockSpec(memory_space=pltpu.SMEM)] + vmem(len(operands)),
        out_specs=pl.BlockSpec(memory_space=pl.ANY),
        scratch_shapes=[
            pltpu.VMEM((2 * NB, c), F32),
            pltpu.VMEM((2 * NB, 2 * NB), F32),
            pltpu.VMEM((r, 2 * NB), F32),
            pltpu.VMEM((r, 6 * NB), BF16),
            pltpu.VMEM((6 * NB, c), BF16),
            pltpu.VMEM((r, c), F32),
            pltpu.SemaphoreType.DMA((STEPS,)),
        ],
        compiler_params=pltpu.CompilerParams(vmem_limit_bytes=32 * 1024 * 1024),
        cost_estimate=cost(5_000_000_000, 18_000_000),
        name="update",
    )(info, *operands)


STEPS = 5


def place(core, p, q):
    return p * 8 + q * 2 if core == 0 else q * 8 + p * 2 + 1


BOTH = ("row", "col")


def whole_permute(v, axis, pairs):
    stride, size = (8, 256) if axis == BOTH else (1, 32)
    to = dict(pairs)
    back = {b: a for a, b in pairs}
    for b in list(back):
        if b not in to:
            a = b
            while a in back:
                a = back[a]
            to[b] = a
    real = dict(pairs)
    for i in range(size):
        j = i ^ stride
        if i in to:
            continue
        if j not in to:
            to[i], to[j] = j, i
        elif j not in real:
            to[i], to[j] = to[j], i
        else:
            k = next(a for a, b in to.items() if b == j)
            assert k not in real
            to[i], to[k] = j, i
    return lax.ppermute(v, axis, sorted(to.items()))


def pick(i, *values):
    out = values[-1]
    for n in range(len(values) - 2, -1, -1):
        out = jnp.where(i == n, values[n], out)
    return out


def local(kernel):
    row = lax.axis_index("row")
    z = lax.axis_index("col")
    y, x, core = row // 8, row // 2 % 4, row % 2
    p = jnp.where(core == 0, y, x)
    q = jnp.where(core == 0, x, y)
    info = jnp.stack([y, x, row, z]).astype(jnp.int32)

    own = kernel[:NB, :NB]
    other = whole_permute(own, BOTH, [(r * 8 + a, r * 8 + 1 - a) for r in (0, 1) for a in (0, 1)])
    corner = jnp.where(z == 0, jnp.concatenate([own, other], 1), jnp.concatenate([other, own], 1))
    got = [
        whole_permute(corner, BOTH, [(r * 8 + a, r * 8 + b) for r in (0, 1) for a, b in ((0, 8 - n), (1, 1 + n))])
        for n in (3, 2, 1)
    ]
    corner = pick(z, corner, corner, got[2], got[1], got[0], got[0], got[1], got[2])
    first = kernel[:, :NB]
    corner, first = lax.optimization_barrier((corner, first))
    got = [
        whole_permute(corner, "row", [(place(c, 0, 0), place(c, 0, n)) for c in (0, 1)]) for n in (2, 1, 3)
    ]
    corner = pick(q, corner, got[1], got[0], got[2])
    got = [
        whole_permute(corner, "row", [(place(c, 0, i), place(c, n, i)) for c in (0, 1) for i in range(4)])
        for n in (2, 1, 3)
    ]
    corner = pick(p, corner, got[1], got[0], got[2])
    swap = lambda v: lax.ppermute(v, "row", [(i, i ^ 1) for i in range(32)])
    corner_other = swap(corner)

    mesh_line = lambda pairs: [(r * 8 + a, r * 8 + b) for r in range(32) for a, b in pairs]
    far = whole_permute(first, BOTH, mesh_line(((0, 4), (1, 5))))
    half = jnp.where((z == 4) | (z == 5), far, first)
    near = whole_permute(half, BOTH, mesh_line(((0, 2), (1, 3), (4, 6), (5, 7))))
    half = jnp.where((z % 4) < 2, half, near)
    half_other = whole_permute(half, BOTH, mesh_line([(i, i ^ 1) for i in range(8)]))

    w = kernel.shape[1] // 4
    quarters = [kernel[:NB, j * w : (j + 1) * w] for j in range(4)]
    got = [
        whole_permute(quarters[j], "row", [(place(c, 0, 0), place(c, j, 0)) for c in (0, 1)]) for j in (2, 1, 3)
    ]
    quarter = pick(p, quarters[0], got[1], got[0], got[2])
    got = [
        whole_permute(quarter, "row", [(place(c, j, 0), place(c, j, n)) for c in (0, 1) for j in range(4)])
        for n in (2, 1, 3)
    ]
    quarter = pick(q, quarter, got[1], got[0], got[2])
    slots = [quarter] + [
        lax.ppermute(
            quarter,
            "row",
            [(place(c, j, i), place(c, (j + n) % 4, i)) for c in (0, 1) for j in range(4) for i in range(4)],
        )
        for n in (1, 2, 3)
    ]

    l0, w0, s = kernel_call(factor_first, "factor_first", [(2 * NB, NB), (NB, NB), (NB, NB)], 1)(
        core.astype(jnp.int32)[None], corner, corner_other
    )
    s, slots = lax.optimization_barrier((s, slots))
    others = [swap(v) for v in slots]
    l1, w1 = kernel_call(factor_second, "factor_second", [(NB, NB), (NB, 2 * NB)])(s, l0, w0)
    return update(info, kernel, [half, half_other], slots, others, l0, w0, l1, w1)


def kernel_call(body, name, shapes, scalars=0):
    def call(*operands):
        return pl.pallas_call(
            body,
            in_specs=[pl.BlockSpec(memory_space=pltpu.SMEM)] * scalars + vmem(len(operands) - scalars),
            out_specs=vmem(len(shapes)),
            out_shape=[sds(*shape) for shape in shapes],
            compiler_params=pltpu.CompilerParams(vmem_limit_bytes=4 * 1024 * 1024),
            cost_estimate=cost(1_000_000_000, 1_000_000),
            name=name,
        )(*operands)

    return call


def solution(mesh):
    return jax.shard_map(
        local,
        mesh=mesh,
        in_specs=(P("row", "col"),),
        out_specs=P("row", "col"),
        check_vma=False,
    )
```
